32 devices in a mesh: groups: 2 (over y), expert: 4 (over z), dp: 2 (over x), pair: 2 (over core).
Axes of the slice: x: 2, y: 2, z: 4, core: 2. Of those that a mesh axis runs over, the one named last changes fastest.
Arguments:
- tokens: bfloat16 [4096, 2048], P(('groups', 'expert', 'dp', 'pair')), parts along dimension 0, may hold values from -6 to 6
- expert_ids: int32 [4096, 2], P(('groups', 'expert', 'dp', 'pair')), parts along dimension 0, may hold values from 0 to 7, all different within a row; in each aligned block of 128 rows (0 to 127, 128 to 255, ...) at most 36 rows name the same one
- gate_weights: float32 [4096, 2], P(('groups', 'expert', 'dp', 'pair')), parts along dimension 0, may hold values from 0.1 to 1
- upstream: bfloat16 [4096, 2048], P(('groups', 'expert', 'dp', 'pair')), parts along dimension 0, may hold values from -6 to 6
- w_gate: bfloat16 [8, 2048, 1408], P(('expert', 'pair'), 'dp'), may hold values from -0.125 to 0.125
- w_up: bfloat16 [8, 2048, 1408], P(('expert', 'pair'), 'dp'), may hold values from -0.125 to 0.125
- w_down: bfloat16 [8, 1408, 2048], P(('expert', 'pair'), 'dp'), may hold values from -0.15625 to 0.15625
Outputs:
- out: bfloat16 [4096, 2048], P(('groups', 'expert', 'dp', 'pair')), parts along dimension 0
- d_tokens: bfloat16 [4096, 2048], P(('groups', 'expert', 'dp', 'pair')), parts along dimension 0
- d_gates: float32 [4096, 2], P(('groups', 'expert', 'dp', 'pair')), parts along dimension 0
- grad_gate: bfloat16 [16, 2048, 1408], P(('groups', 'expert', 'pair'), 'dp'), parts along dimension 0
- grad_up: bfloat16 [16, 2048, 1408], P(('groups', 'expert', 'pair'), 'dp'), parts along dimension 0
- grad_down: bfloat16 [16, 1408, 2048], P(('groups', 'expert', 'pair'), 'dp'), parts along dimension 0
The draws below stay inside these ranges and needn't reach their ends.
There are 2 independent parts, one for each index of `groups`. The reference program is written for one: setup_inputs(seed, part) draws one part's arguments, and reference() takes and returns one part's arrays. A program takes and returns all parts, laid end to end along the dimension named above; an argument that names none is the same for every part. Nothing has to cross between parts.
Inputs may be any that keep to these rules, and one draw needn't show every extreme that they name: `expert_ids`: each token names 2 different experts; the 128 tokens of one device name one expert at most 36 times, and exactly 36 times in some blocks.
All inputs are finite; a program needn't handle non-finite values.
Results may differ from the reference program's by a relative error of at most 0.009.
Values may be sent and summed in bfloat16 or wider, within the bound.
A program may use at most 128 MiB of HBM per device.

```python
import math
import jax
import jax.numpy as jnp
import numpy as np
from jax import lax

D = 2048
FF = 1408
TOP = 2
TOK_DEV = 128
EXPERTS = 8
CAP = 36
TOKENS = 2048
N_EXPERT = 4
N_DP = 2
N_PAIR = 2


def shard_levels(key, shape, split, least, high):
    gain = 1.0
    for dim, shards_of in split:
        heights = jax.random.uniform(jax.random.fold_in(jax.random.fold_in(key, 6), dim), (shards_of,), jnp.float32, least / len(split), high / len(split))
        gain = gain * jnp.repeat(jnp.exp(heights), shape[dim] // shards_of).reshape((-1,) + (1,) * (len(shape) - 1 - dim))
    return gain


def shared_out(stream_key, own, number, rows, number_of, top, limit, lean):
    sequence = jax.random.permutation(stream_key, number_of)
    heavy_load, common = shares(number_of, rows * top, limit, lean, True), shares(number_of, rows * top, limit, lean, False)
    places = jnp.arange(number_of)

    def named(sizes, rotation):
        used = int((sizes > 0).sum())
        fixed = max(1, used // 4)
        shifted = fixed + (places - fixed + rotation * (used - fixed)) % max(1, number_of - fixed)
        return jnp.zeros((number_of,), jnp.int32).at[sequence[jnp.where(places < fixed, places, shifted)]].set(jnp.asarray(sizes, jnp.int32))

    sizes = jnp.where(number % 4 == 0, named(heavy_load, number // 4), named(common, number - number // 4 - 1))
    mixed = jax.random.permutation(jax.random.fold_in(own, 3), number_of)
    donor, sink = mixed[0:number_of // 2 * 2:2], mixed[1:number_of // 2 * 2:2]
    room = jnp.minimum(sizes[donor] - 1, limit - sizes[sink]) // 2
    room = jnp.where((donor == sequence[0]) | (sink == sequence[0]) | (sizes[sink] == 0), 0, jnp.maximum(room, 0))
    shifted = jax.random.randint(jax.random.fold_in(own, 4), (number_of // 2,), 0, 1 << 20) % (room + 1)
    sizes = sizes.at[donor].add(-shifted).at[sink].add(shifted)
    items = jnp.searchsorted(jnp.cumsum(sizes), jnp.arange(rows * top), side="right").astype(jnp.int32)
    listing = items.reshape(top, rows).T
    listing = listing[jax.random.permutation(jax.random.fold_in(own, 1), rows)]
    rotation = jax.random.randint(jax.random.fold_in(own, 2), (rows, 1), 0, top)
    return jnp.take_along_axis(listing, (jnp.arange(top)[None, :] + rotation) % top, axis=1)


def shares(amount, total, limit, lean, full):
    weights = [(1 << 20) // math.isqrt(grade ** lean) + 1 for grade in range(1, amount + 1)]
    largest = limit if full else min(limit, max(-(-total // amount), total * weights[0] // sum(weights)))
    least = 1 if total - largest >= amount - 1 else 0
    given, surplus = [largest] + [least] * (amount - 1), total - largest - least * (amount - 1)
    while surplus > 0:
        free = [i for i in range(1, amount) if given[i] < largest] or [i for i in range(1, amount) if given[i] < limit]
        mass, left = sum([weights[i] for i in free]), surplus
        for i in free:
            more = min(limit - given[i], max(1, left * weights[i] // mass), surplus)
            given[i] = given[i] + more
            surplus = surplus - more
    return np.array(given)


def noise(key, extent, width, most, shards=(), held_as=jnp.bfloat16):
    values = width * jax.random.normal(key, extent, jnp.float32)
    if shards:
        values = values * shard_levels(key, extent, shards, -0.22, 0.18)
    return jnp.clip(values, -most, most).astype(held_as)


def setup_inputs(seed: int = 0, part: int = 0) -> dict:
    key_list = jax.random.split(jax.random.key(seed), 8)
    part_keys = jax.random.split(jax.random.fold_in(key_list[7], part), 8)
    tokens = noise(part_keys[0], (TOKENS, D), 1.0, 6.0, ((0, 16),))
    expert_ids_keys = jax.random.split(jax.random.fold_in(part_keys[1], 1), TOKENS // TOK_DEV)
    expert_ids_turns = jax.random.permutation(jax.random.fold_in(part_keys[1], 3), TOKENS // TOK_DEV)
    expert_ids = jax.vmap(lambda own, number: shared_out(jax.random.fold_in(part_keys[1], 2), own, number, TOK_DEV, EXPERTS, TOP, CAP, 2))(expert_ids_keys, expert_ids_turns).reshape((TOKENS, TOP))
    gate_weights = jnp.clip(jnp.exp(math.log(1.0) - 2.3025851 * jax.random.uniform(part_keys[2], (TOKENS, TOP), jnp.float32) ** shard_levels(part_keys[2], (TOKENS, TOP), ((0, 16),), -0.2, 0.2)), 0.1, 1.0)
    upstream = noise(part_keys[3], (TOKENS, D), 1.0, 6.0, ((0, 16),))
    w_gate = noise(key_list[4], (EXPERTS, D, FF), D ** -0.5, 0.125, ((0, 8), (1, 2)))
    w_up = noise(key_list[5], (EXPERTS, D, FF), D ** -0.5, 0.125, ((0, 8), (1, 2)))
    w_down = noise(key_list[6], (EXPERTS, FF, D), FF ** -0.5, 0.15625, ((0, 8), (1, 2)))
    return dict(tokens=tokens, expert_ids=expert_ids, gate_weights=gate_weights, upstream=upstream, w_gate=w_gate, w_up=w_up, w_down=w_down)


def expert_pass(inputs, scaled, gate_w, up_w, down_w):
    gate_pre = jnp.dot(inputs, gate_w, preferred_element_type=jnp.float32)
    up_pre = jnp.dot(inputs, up_w, preferred_element_type=jnp.float32)
    squash = jax.nn.sigmoid(gate_pre)
    active = gate_pre * squash
    hidden = (active * up_pre).astype(jnp.bfloat16)
    output = jnp.dot(hidden, down_w, preferred_element_type=jnp.float32).astype(jnp.bfloat16)
    hidden_grad = jnp.dot(scaled, down_w.T, preferred_element_type=jnp.float32)
    gate_grad = (hidden_grad * up_pre * (squash + active * (1.0 - squash))).astype(jnp.bfloat16)
    up_grad = (hidden_grad * active).astype(jnp.bfloat16)
    input_grad = (jnp.dot(gate_grad, gate_w.T, preferred_element_type=jnp.float32)
                  + jnp.dot(up_grad, up_w.T, preferred_element_type=jnp.float32)).astype(jnp.bfloat16)
    return hidden, output, gate_grad, up_grad, input_grad


def by_replica(values):
    return values.reshape(N_EXPERT, N_DP, N_PAIR * CAP, values.shape[1]).astype(jnp.float32)


def replica_sum(first_op, second_op):
    products = jnp.einsum("adrk,adrf->dkf", by_replica(first_op), by_replica(second_op))
    rounded = lax.optimization_barrier(products.astype(jnp.bfloat16))
    return jnp.sum(rounded.astype(jnp.float32), 0).astype(jnp.bfloat16)


def reference(tokens, expert_ids, gate_weights, upstream, w_gate, w_up, w_down):
    device_count = TOKENS // TOK_DEV
    per_device = TOK_DEV * TOP
    all_rows = TOKENS * TOP
    device_ids = expert_ids.reshape(device_count, per_device)
    onehot = (device_ids[:, :, None] == jnp.arange(EXPERTS, dtype=jnp.int32)[None, None, :]).astype(jnp.int32)
    position = jnp.sum(jnp.cumsum(onehot, 1) * onehot, 2) - 1
    device_rows = jnp.arange(device_count, dtype=jnp.int32)[:, None]
    columns = (device_rows * CAP + position).astype(jnp.int32)
    row_index = jnp.arange(all_rows, dtype=jnp.int32).reshape(device_count, per_device)
    slot_table = jnp.full((EXPERTS, device_count * CAP), all_rows, jnp.int32).at[device_ids, columns].set(row_index)
    zero_row = jnp.zeros((1, D), jnp.bfloat16)
    token_ext = jnp.concatenate([tokens, zero_row], 0)
    scaled = (gate_weights[:, :, None] * upstream.astype(jnp.float32)[:, None, :]).astype(jnp.bfloat16)
    scaled_ext = jnp.concatenate([scaled.reshape(all_rows, D), zero_row], 0)

    def one_expert(expert_id):
        slot_rows = slot_table[expert_id]
        rows_in = token_ext[slot_rows // TOP]
        grads_in = scaled_ext[slot_rows]
        hidden, output, gate_grad, up_grad, input_grad = expert_pass(
            rows_in, grads_in, w_gate[expert_id], w_up[expert_id], w_down[expert_id])
        grad_g = replica_sum(rows_in, gate_grad)
        grad_u = replica_sum(rows_in, up_grad)
        grad_d = replica_sum(hidden, grads_in)
        return output, input_grad, grad_g, grad_u, grad_d

    outputs, input_grads, grad_gate, grad_up, grad_down = lax.map(one_expert, jnp.arange(EXPERTS, dtype=jnp.int32))
    flat_slots = slot_table.reshape(-1)
    out_rows = jnp.zeros((all_rows + 1, D), jnp.bfloat16).at[flat_slots].set(outputs.reshape(-1, D))[:all_rows]
    grad_rows = jnp.zeros((all_rows + 1, D), jnp.bfloat16).at[flat_slots].set(input_grads.reshape(-1, D))[:all_rows]
    out_rows = out_rows.reshape(TOKENS, TOP, D).astype(jnp.float32)
    grad_rows = grad_rows.reshape(TOKENS, TOP, D).astype(jnp.float32)
    out = jnp.sum(gate_weights[:, :, None] * out_rows, 1).astype(jnp.bfloat16)
    d_gates = jnp.sum(upstream.astype(jnp.float32)[:, None, :] * out_rows, 2)
    d_tokens = jnp.sum(grad_rows, 1).astype(jnp.bfloat16)
    return (out, d_tokens, d_gates, grad_gate, grad_up, grad_down)
```

```python
import jax
import jax.numpy as jnp
from jax import lax
from jax.sharding import PartitionSpec as P

F32 = jnp.float32
BF16 = jnp.bfloat16


def shift(value, axis, step):
    size = lax.axis_size(axis)
    return lax.ppermute(value, axis, [(i, (i + step) % size) for i in range(size)])


def gather_weight(weight):
    rows, cols = weight.shape
    n_replica = lax.axis_size("dp")
    n_group = lax.axis_size("groups")
    me = lax.axis_index("dp")
    group = lax.axis_index("groups")
    if rows % (16 * n_group):
        n_group, group = 1, 0
    share = rows // n_group
    mine = lax.dynamic_slice_in_dim(weight, group * share, share, 0)
    full = jnp.zeros((n_replica * rows, cols), weight.dtype)
    full = lax.dynamic_update_slice_in_dim(full, weight, me * rows, 0)
    for step in range(1, n_replica):
        owner = lax.rem(me - step + n_replica, n_replica)
        piece = shift(mine, "dp", step)
        full = lax.dynamic_update_slice_in_dim(full, piece, owner * rows + group * share, 0)
        for hop in range(1, n_group):
            other = shift(piece, "groups", hop)
            origin = lax.rem(group - hop + n_group, n_group)
            full = lax.dynamic_update_slice_in_dim(full, other, owner * rows + origin * share, 0)
    return full


def dot(a, b, a_dim=1, b_dim=0):
    return lax.dot_general(a, b, (((a_dim,), (b_dim,)), ((), ())), preferred_element_type=F32)


def per_device(tokens, expert_ids, gate_weights, upstream, w_gate, w_up, w_down):
    tok_rows, model_width = tokens.shape
    chosen = expert_ids.shape[1]
    n_expert = lax.axis_size("expert")
    n_pair = lax.axis_size("pair")
    n_replica = lax.axis_size("dp")
    me = lax.axis_index("dp")
    experts = n_expert * n_pair
    capacity = max(2, tok_rows * chosen * 9 // (experts * 8))
    row_count = tok_rows * chosen
    slots = experts * capacity

    full_gate = gather_weight(w_gate[0])
    full_up = gather_weight(w_up[0])
    full_down = gather_weight(w_down[0])

    flat_ids = expert_ids.reshape(row_count)
    order = jnp.arange(row_count, dtype=jnp.int32)
    same = (flat_ids[:, None] == flat_ids[None, :]) & (order[None, :] < order[:, None])
    position = jnp.sum(same.astype(jnp.int32), 1)
    slot_index = (flat_ids * capacity + position).reshape(tok_rows, chosen)
    slot_ids = jnp.arange(slots, dtype=jnp.int32)
    picks = [(slot_ids[:, None] == slot_index[None, :, k]).astype(BF16) for k in range(chosen)]
    any_pick = sum(picks[1:], picks[0])
    wide = upstream.astype(F32)
    send_rows = dot(any_pick, tokens).astype(BF16)
    send_grads = sum(
        dot(picks[k], (gate_weights[:, k : k + 1] * wide).astype(BF16)) for k in range(chosen)
    ).astype(BF16)

    def exchange(value):
        value = value.reshape(experts, capacity, model_width)
        value = lax.all_to_all(value, ("expert", "pair"), split_axis=0, concat_axis=0, tiled=True)
        return value.reshape(slots, model_width)

    rows = exchange(send_rows)
    grads = exchange(send_grads)
    gate_pre = dot(rows, full_gate)
    up_pre = dot(rows, full_up)
    squash = jax.nn.sigmoid(gate_pre)
    active = gate_pre * squash
    hidden = (active * up_pre).astype(BF16)
    output = dot(hidden, full_down).astype(BF16)
    back_out = exchange(output)
    hidden_grad = dot(grads, full_down, 1, 1)
    gate_grad = (hidden_grad * up_pre * (squash + active * (1.0 - squash))).astype(BF16)
    up_grad = (hidden_grad * active).astype(BF16)
    input_grad = (dot(gate_grad, full_gate, 1, 1) + dot(up_grad, full_up, 1, 1)).astype(BF16)
    back_grad = exchange(input_grad)

    def part(value, index):
        width = value.shape[1] // n_replica
        return lax.dynamic_slice_in_dim(value, index * width, width, 1)

    sum_gate = dot(part(rows, me), gate_grad, 0, 0)
    sum_up = dot(part(rows, me), up_grad, 0, 0)
    sum_down = dot(part(hidden, me), grads, 0, 0)
    for step in range(1, n_replica):
        target = lax.rem(me + step, n_replica)
        their_grads = shift(grads, "dp", step)
        their_rows = shift(part(rows, target), "dp", step)
        their_hidden = shift(part(hidden, target), "dp", step)
        their_gate = shift(gate_grad, "dp", step)
        their_up = shift(up_grad, "dp", step)
        sum_down += dot(their_hidden, their_grads, 0, 0)
        sum_gate += dot(their_rows, their_gate, 0, 0)
        sum_up += dot(their_rows, their_up, 0, 0)

    out_rows = [dot(picks[k], back_out, 0, 0) for k in range(chosen)]
    result = sum(gate_weights[:, k : k + 1] * out_rows[k] for k in range(chosen)).astype(BF16)
    d_gates = jnp.stack([jnp.sum(wide * out_rows[k], 1) for k in range(chosen)], 1)
    d_tokens = dot(any_pick, back_grad, 0, 0).astype(BF16)
    return (
        result,
        d_tokens,
        d_gates,
        sum_gate.astype(BF16)[None],
        sum_up.astype(BF16)[None],
        sum_down.astype(BF16)[None],
    )


def solution(mesh):
    rows = P(("groups", "expert", "dp", "pair"), None)
    weights = P(("expert", "pair"), "dp", None)
    summed = P(("groups", "expert", "pair"), "dp", None)
    return jax.shard_map(
        per_device,
        mesh=mesh,
        in_specs=(rows, rows, rows, rows, weights, weights, weights),
        out_specs=(rows, rows, rows, summed, summed, summed),
        check_vma=False,
    )
```

```python
import jax
import jax.numpy as jnp
from jax import lax
from jax.sharding import PartitionSpec as P

F32 = jnp.float32
BF16 = jnp.bfloat16


def shift(value, axis, step):
    size = lax.axis_size(axis)
    return lax.ppermute(value, axis, [(i, (i + step) % size) for i in range(size)])


def pieces_of(weight):
    rows = weight.shape[0]
    n_group = lax.axis_size("groups")
    group = lax.axis_index("groups")
    if rows % (16 * n_group):
        n_group, group = 1, 0
    share = rows // n_group
    chunks = 2 if share % 32 == 0 else 1
    size = share // chunks
    return [
        lax.dynamic_slice_in_dim(weight, group * share + c * size, size, 0) for c in range(chunks)
    ]


def fetch(mine):
    return [[shift(chunk, "dp", step) for chunk in mine] for step in range(1, lax.axis_size("dp"))]


def gather_weight(weight, fetched):
    rows, cols = weight.shape
    n_replica = lax.axis_size("dp")
    me = lax.axis_index("dp")
    size = fetched[0][0].shape[0]
    share = size * len(fetched[0])
    n_group = rows // share
    group = lax.axis_index("groups") if n_group > 1 else 0
    full = jnp.zeros((n_replica * rows, cols), weight.dtype)
    full = lax.dynamic_update_slice_in_dim(full, weight, me * rows, 0)
    for step in range(1, n_replica):
        owner = lax.rem(me - step + n_replica, n_replica)
        for c, piece in enumerate(fetched[step - 1]):
            base = owner * rows + c * size
            full = lax.dynamic_update_slice_in_dim(full, piece, base + group * share, 0)
            for hop in range(1, n_group):
                other = shift(piece, "groups", hop)
                origin = lax.rem(group - hop + n_group, n_group)
                full = lax.dynamic_update_slice_in_dim(full, other, base + origin * share, 0)
    return full


def dot(a, b, a_dim=1, b_dim=0):
    return lax.dot_general(a, b, (((a_dim,), (b_dim,)), ((), ())), preferred_element_type=F32)


def per_device(tokens, expert_ids, gate_weights, upstream, w_gate, w_up, w_down):
    tok_rows, model_width = tokens.shape
    chosen = expert_ids.shape[1]
    n_expert = lax.axis_size("expert")
    n_pair = lax.axis_size("pair")
    n_replica = lax.axis_size("dp")
    me = lax.axis_index("dp")
    experts = n_expert * n_pair
    capacity = max(2, tok_rows * chosen * 9 // (experts * 8))
    row_count = tok_rows * chosen
    slots = experts * capacity

    gate_mine, up_mine, down_mine = (pieces_of(w[0]) for w in (w_gate, w_up, w_down))
    gate_mine, expert_ids = lax.optimization_barrier((gate_mine, expert_ids))
    gate_fetched, up_fetched = fetch(gate_mine), fetch(up_mine)

    flat_ids = expert_ids.reshape(row_count)
    order = jnp.arange(row_count, dtype=jnp.int32)
    same = (flat_ids[:, None] == flat_ids[None, :]) & (order[None, :] < order[:, None])
    position = jnp.sum(same.astype(jnp.int32), 1)
    slot_index = (flat_ids * capacity + position).reshape(tok_rows, chosen)
    slot_ids = jnp.arange(slots, dtype=jnp.int32)
    picks = [(slot_ids[:, None] == slot_index[None, :, k]).astype(BF16) for k in range(chosen)]
    any_pick = sum(picks[1:], picks[0])
    wide = upstream.astype(F32)
    send_rows = dot(any_pick, tokens).astype(BF16)
    send_grads = sum(
        dot(picks[k], (gate_weights[:, k : k + 1] * wide).astype(BF16)) for k in range(chosen)
    ).astype(BF16)

    def exchange(value):
        value = value.reshape(experts, capacity, model_width)
        value = lax.all_to_all(value, ("expert", "pair"), split_axis=0, concat_axis=0, tiled=True)
        return value.reshape(slots, model_width)

    def part(value, index):
        width = value.shape[1] // n_replica
        return lax.dynamic_slice_in_dim(value, index * width, width, 1)

    def to_replicas(value, split=False):
        targets = [lax.rem(me + step, n_replica) for step in range(n_replica)]
        sent = [part(value, target) if split else value for target in targets]
        return sent[:1] + [shift(sent[step], "dp", step) for step in range(1, n_replica)]

    rows = exchange(send_rows)
    rows, send_grads, down_mine, gate_fetched[0][-1] = lax.optimization_barrier(
        (rows, send_grads, down_mine, gate_fetched[0][-1])
    )
    grads = exchange(send_grads)
    down_fetched = fetch(down_mine)
    full_gate = gather_weight(w_gate[0], gate_fetched)
    full_up = gather_weight(w_up[0], up_fetched)
    full_down = gather_weight(w_down[0], down_fetched)
    all_rows = to_replicas(rows, split=True)
    all_grads = to_replicas(grads)
    gate_pre = dot(rows, full_gate)
    up_pre = dot(rows, full_up)
    squash = jax.nn.sigmoid(gate_pre)
    active = gate_pre * squash
    hidden, full_down = lax.optimization_barrier(((active * up_pre).astype(BF16), full_down))
    output = dot(hidden, full_down).astype(BF16)
    back_out = exchange(output)
    all_rows, held_grads = lax.optimization_barrier((all_rows, grads))
    hidden_grad = dot(held_grads, full_down, 1, 1)
    gate_grad = (hidden_grad * up_pre * (squash + active * (1.0 - squash))).astype(BF16)
    up_grad = (hidden_grad * active).astype(BF16)
    all_gate = to_replicas(gate_grad)
    all_up = to_replicas(up_grad)
    all_hidden = to_replicas(hidden, split=True)
    all_grads, held_gate = lax.optimization_barrier((all_grads, gate_grad))
    input_grad = (dot(held_gate, full_gate, 1, 1) + dot(up_grad, full_up, 1, 1)).astype(BF16)
    back_grad = exchange(input_grad)

    joined = [jnp.concatenate(v, 0) for v in (all_rows, all_hidden, all_gate, all_up, all_grads)]
    all_rows, all_hidden, all_gate, all_up, all_grads = joined
    sum_gate = dot(all_rows, all_gate, 0, 0)
    sum_up = dot(all_rows, all_up, 0, 0)
    sum_down = dot(all_hidden, all_grads, 0, 0)

    out_rows = [dot(picks[k], back_out, 0, 0) for k in range(chosen)]
    result = sum(gate_weights[:, k : k + 1] * out_rows[k] for k in range(chosen)).astype(BF16)
    d_gates = jnp.stack([jnp.sum(wide * out_rows[k], 1) for k in range(chosen)], 1)
    d_tokens = dot(any_pick, back_grad, 0, 0).astype(BF16)
    return (
        result,
        d_tokens,
        d_gates,
        sum_gate.astype(BF16)[None],
        sum_up.astype(BF16)[None],
        sum_down.astype(BF16)[None],
    )


def solution(mesh):
    rows = P(("groups", "expert", "dp", "pair"), None)
    weights = P(("expert", "pair"), "dp", None)
    summed = P(("groups", "expert", "pair"), "dp", None)
    return jax.shard_map(
        per_device,
        mesh=mesh,
        in_specs=(rows, rows, rows, rows, weights, weights, weights),
        out_specs=(rows, rows, rows, summed, summed, summed),
        check_vma=False,
    )
```

```python
import jax
import jax.numpy as jnp
from jax import lax
from jax.sharding import PartitionSpec as P

F32 = jnp.float32
BF16 = jnp.bfloat16


def shift(value, axis, step):
    size = lax.axis_size(axis)
    return lax.ppermute(value, axis, [(i, (i + step) % size) for i in range(size)])


def pieces_of(weight):
    rows = weight.shape[0]
    n_group = lax.axis_size("groups")
    group = lax.axis_index("groups")
    if rows % (16 * n_group):
        n_group, group = 1, 0
    share = rows // n_group
    chunks = 2 if share % 32 == 0 else 1
    size = share // chunks
    return [
        lax.dynamic_slice_in_dim(weight, group * share + c * size, size, 0) for c in range(chunks)
    ]


def fetch(mine):
    return [[shift(chunk, "dp", step) for chunk in mine] for step in range(1, lax.axis_size("dp"))]


def gather_weight(weight, fetched):
    rows, cols = weight.shape
    n_replica = lax.axis_size("dp")
    me = lax.axis_index("dp")
    size = fetched[0][0].shape[0]
    share = size * len(fetched[0])
    n_group = rows // share
    group = lax.axis_index("groups") if n_group > 1 else 0
    full = jnp.zeros((n_replica * rows, cols), weight.dtype)
    full = lax.dynamic_update_slice_in_dim(full, weight, me * rows, 0)
    for step in range(1, n_replica):
        owner = lax.rem(me - step + n_replica, n_replica)
        for c, piece in enumerate(fetched[step - 1]):
            base = owner * rows + c * size
            full = lax.dynamic_update_slice_in_dim(full, piece, base + group * share, 0)
            for hop in range(1, n_group):
                other = shift(piece, "groups", hop)
                origin = lax.rem(group - hop + n_group, n_group)
                full = lax.dynamic_update_slice_in_dim(full, other, base + origin * share, 0)
    return full


def dot(a, b, a_dim=1, b_dim=0):
    return lax.dot_general(a, b, (((a_dim,), (b_dim,)), ((), ())), preferred_element_type=F32)


def per_device(tokens, expert_ids, gate_weights, upstream, w_gate, w_up, w_down):
    tok_rows, model_width = tokens.shape
    chosen = expert_ids.shape[1]
    n_expert = lax.axis_size("expert")
    n_pair = lax.axis_size("pair")
    n_replica = lax.axis_size("dp")
    me = lax.axis_index("dp")
    experts = n_expert * n_pair
    capacity = max(2, tok_rows * chosen * 9 // (experts * 8))
    row_count = tok_rows * chosen
    slots = experts * capacity

    gate_mine, up_mine, down_mine = (pieces_of(w[0]) for w in (w_gate, w_up, w_down))
    gate_mine, expert_ids = lax.optimization_barrier((gate_mine, expert_ids))
    gate_fetched, up_fetched = fetch(gate_mine), fetch(up_mine)

    flat_ids = expert_ids.reshape(row_count)
    order = jnp.arange(row_count, dtype=jnp.int32)
    same = (flat_ids[:, None] == flat_ids[None, :]) & (order[None, :] < order[:, None])
    position = jnp.sum(same.astype(jnp.int32), 1)
    slot_index = (flat_ids * capacity + position).reshape(tok_rows, chosen)
    slot_ids = jnp.arange(slots, dtype=jnp.int32)
    picks = [(slot_ids[:, None] == slot_index[None, :, k]).astype(BF16) for k in range(chosen)]
    any_pick = sum(picks[1:], picks[0])
    wide = upstream.astype(F32)
    send_rows = dot(any_pick, tokens).astype(BF16)
    send_grads = sum(
        dot(picks[k], (gate_weights[:, k : k + 1] * wide).astype(BF16)) for k in range(chosen)
    ).astype(BF16)

    def exchange(value):
        value = value.reshape(experts, capacity, model_width)
        value = lax.all_to_all(value, ("expert", "pair"), split_axis=0, concat_axis=0, tiled=True)
        return value.reshape(slots, model_width)

    def part(value, index):
        width = value.shape[1] // n_replica
        return lax.dynamic_slice_in_dim(value, index * width, width, 1)

    def to_replicas(value, split=False):
        targets = [lax.rem(me + step, n_replica) for step in range(n_replica)]
        sent = [part(value, target) if split else value for target in targets]
        return sent[:1] + [shift(sent[step], "dp", step) for step in range(1, n_replica)]

    rows = exchange(send_rows)
    rows, send_grads, down_mine, gate_fetched = lax.optimization_barrier(
        (rows, send_grads, down_mine, gate_fetched)
    )
    up_fetched, _ = lax.optimization_barrier((up_fetched, rows))
    held_rows, grads = lax.optimization_barrier((rows, exchange(send_grads)))
    down_fetched = fetch(down_mine)
    full_gate = gather_weight(w_gate[0], gate_fetched)
    full_up = gather_weight(w_up[0], up_fetched)
    full_down = gather_weight(w_down[0], down_fetched)
    all_rows = to_replicas(rows, split=True)
    all_grads = to_replicas(grads)
    gate_pre = dot(held_rows, full_gate)
    up_pre = dot(held_rows, full_up)
    squash = jax.nn.sigmoid(gate_pre)
    active = gate_pre * squash
    hidden, full_down = lax.optimization_barrier(((active * up_pre).astype(BF16), full_down))
    output = dot(hidden, full_down).astype(BF16)
    back_out = exchange(output)
    all_rows, held_grads = lax.optimization_barrier((all_rows, grads))
    hidden_grad = dot(held_grads, full_down, 1, 1)
    gate_grad = (hidden_grad * up_pre * (squash + active * (1.0 - squash))).astype(BF16)
    up_grad = (hidden_grad * active).astype(BF16)
    all_gate = to_replicas(gate_grad)
    all_up = to_replicas(up_grad)
    all_hidden = to_replicas(hidden, split=True)
    all_grads, held_gate = lax.optimization_barrier((all_grads, gate_grad))
    input_grad = (dot(held_gate, full_gate, 1, 1) + dot(up_grad, full_up, 1, 1)).astype(BF16)
    back_grad = exchange(input_grad)

    joined = [jnp.concatenate(v, 0) for v in (all_rows, all_hidden, all_gate, all_up, all_grads)]
    all_rows, all_hidden, all_gate, all_up, all_grads = joined
    sum_gate = dot(all_rows, all_gate, 0, 0)
    sum_up = dot(all_rows, all_up, 0, 0)
    sum_down = dot(all_hidden, all_grads, 0, 0)

    out_rows = [dot(picks[k], back_out, 0, 0) for k in range(chosen)]
    result = sum(gate_weights[:, k : k + 1] * out_rows[k] for k in range(chosen)).astype(BF16)
    d_gates = jnp.stack([jnp.sum(wide * out_rows[k], 1) for k in range(chosen)], 1)
    d_tokens = dot(any_pick, back_grad, 0, 0).astype(BF16)
    return (
        result,
        d_tokens,
        d_gates,
        sum_gate.astype(BF16)[None],
        sum_up.astype(BF16)[None],
        sum_down.astype(BF16)[None],
    )


def solution(mesh):
    rows = P(("groups", "expert", "dp", "pair"), None)
    weights = P(("expert", "pair"), "dp", None)
    summed = P(("groups", "expert", "pair"), "dp", None)
    return jax.shard_map(
        per_device,
        mesh=mesh,
        in_specs=(rows, rows, rows, rows, weights, weights, weights),
        out_specs=(rows, rows, rows, summed, summed, summed),
        check_vma=False,
    )
```

```python
import jax
import jax.numpy as jnp
from jax import lax
from jax.sharding import PartitionSpec as P

F32 = jnp.float32
BF16 = jnp.bfloat16


def shift(value, axis, step):
    size = lax.axis_size(axis)
    return lax.ppermute(value, axis, [(i, (i + step) % size) for i in range(size)])


def pieces_of(weight):
    rows = weight.shape[0]
    n_group = lax.axis_size("groups")
    group = lax.axis_index("groups")
    if rows % (16 * n_group):
        n_group, group = 1, 0
    share = rows // n_group
    chunks = 2 if share % 32 == 0 else 1
    size = share // chunks
    return [
        lax.dynamic_slice_in_dim(weight, group * share + c * size, size, 0) for c in range(chunks)
    ]


def fetch(mine):
    return [[shift(chunk, "dp", step) for chunk in mine] for step in range(1, lax.axis_size("dp"))]


def gather_weight(weight, fetched):
    rows, cols = weight.shape
    n_replica = lax.axis_size("dp")
    me = lax.axis_index("dp")
    size = fetched[0][0].shape[0]
    share = size * len(fetched[0])
    n_group = rows // share
    group = lax.axis_index("groups") if n_group > 1 else 0
    full = jnp.zeros((n_replica * rows, cols), weight.dtype)
    full = lax.dynamic_update_slice_in_dim(full, weight, me * rows, 0)
    for step in range(1, n_replica):
        owner = lax.rem(me - step + n_replica, n_replica)
        for c, piece in enumerate(fetched[step - 1]):
            base = owner * rows + c * size
            full = lax.dynamic_update_slice_in_dim(full, piece, base + group * share, 0)
            for hop in range(1, n_group):
                other = shift(piece, "groups", hop)
                origin = lax.rem(group - hop + n_group, n_group)
                full = lax.dynamic_update_slice_in_dim(full, other, base + origin * share, 0)
    return full


def dot(a, b, a_dim=1, b_dim=0):
    return lax.dot_general(a, b, (((a_dim,), (b_dim,)), ((), ())), preferred_element_type=F32)


def per_device(tokens, expert_ids, gate_weights, upstream, w_gate, w_up, w_down):
    tok_rows, model_width = tokens.shape
    chosen = expert_ids.shape[1]
    n_expert = lax.axis_size("expert")
    n_pair = lax.axis_size("pair")
    n_replica = lax.axis_size("dp")
    me = lax.axis_index("dp")
    experts = n_expert * n_pair
    capacity = max(2, tok_rows * chosen * 9 // (experts * 8))
    row_count = tok_rows * chosen
    slots = experts * capacity

    gate_mine, up_mine, down_mine = (pieces_of(w[0]) for w in (w_gate, w_up, w_down))
    gate_mine, expert_ids = lax.optimization_barrier((gate_mine, expert_ids))
    gate_fetched, up_fetched = fetch(gate_mine), fetch(up_mine)

    flat_ids = expert_ids.reshape(row_count)
    order = jnp.arange(row_count, dtype=jnp.int32)
    same = (flat_ids[:, None] == flat_ids[None, :]) & (order[None, :] < order[:, None])
    position = jnp.sum(same.astype(jnp.int32), 1)
    slot_index = (flat_ids * capacity + position).reshape(tok_rows, chosen)
    slot_ids = jnp.arange(slots, dtype=jnp.int32)
    picks = [(slot_ids[:, None] == slot_index[None, :, k]).astype(BF16) for k in range(chosen)]
    any_pick = sum(picks[1:], picks[0])
    wide = upstream.astype(F32)
    send_rows = dot(any_pick, tokens).astype(BF16)
    send_grads = sum(
        dot(picks[k], (gate_weights[:, k : k + 1] * wide).astype(BF16)) for k in range(chosen)
    ).astype(BF16)

    def exchange(value):
        value = value.reshape(experts, capacity, model_width)
        value = lax.all_to_all(value, ("expert", "pair"), split_axis=0, concat_axis=0, tiled=True)
        return value.reshape(slots, model_width)

    def part(value, index):
        width = value.shape[1] // n_replica
        return lax.dynamic_slice_in_dim(value, index * width, width, 1)

    def to_replicas(value, split=False):
        targets = [lax.rem(me + step, n_replica) for step in range(n_replica)]
        sent = [part(value, target) if split else value for target in targets]
        return sent[:1] + [shift(sent[step], "dp", step) for step in range(1, n_replica)]

    rows = exchange(send_rows)
    rows, send_grads, down_mine, gate_fetched = lax.optimization_barrier(
        (rows, send_grads, down_mine, gate_fetched)
    )
    up_fetched, _ = lax.optimization_barrier((up_fetched, rows))
    grads = exchange(send_grads)
    down_fetched = fetch(down_mine)
    full_gate = gather_weight(w_gate[0], gate_fetched)
    full_up = gather_weight(w_up[0], up_fetched)
    full_down = gather_weight(w_down[0], down_fetched)
    all_rows = to_replicas(rows, split=True)
    all_grads = to_replicas(grads)
    gate_pre = dot(rows, full_gate)
    up_pre = dot(rows, full_up)
    squash = jax.nn.sigmoid(gate_pre)
    active = gate_pre * squash
    hidden, full_down = lax.optimization_barrier(((active * up_pre).astype(BF16), full_down))
    output = dot(hidden, full_down).astype(BF16)
    back_out = exchange(output)
    all_rows, held_grads = lax.optimization_barrier((all_rows, grads))
    hidden_grad = dot(held_grads, full_down, 1, 1)
    gate_grad = (hidden_grad * up_pre * (squash + active * (1.0 - squash))).astype(BF16)
    up_grad = (hidden_grad * active).astype(BF16)
    all_gate = to_replicas(gate_grad)
    all_up = to_replicas(up_grad)
    all_hidden = to_replicas(hidden, split=True)
    input_grad = (dot(gate_grad, full_gate, 1, 1) + dot(up_grad, full_up, 1, 1)).astype(BF16)
    back_grad = exchange(input_grad)

    joined = [jnp.concatenate(v, 0) for v in (all_rows, all_hidden, all_gate, all_up, all_grads)]
    all_rows, all_hidden, all_gate, all_up, all_grads = joined
    sum_gate = dot(all_rows, all_gate, 0, 0)
    sum_up = dot(all_rows, all_up, 0, 0)
    sum_down = dot(all_hidden, all_grads, 0, 0)

    out_rows = [dot(picks[k], back_out, 0, 0) for k in range(chosen)]
    result = sum(gate_weights[:, k : k + 1] * out_rows[k] for k in range(chosen)).astype(BF16)
    d_gates = jnp.stack([jnp.sum(wide * out_rows[k], 1) for k in range(chosen)], 1)
    d_tokens = dot(any_pick, back_grad, 0, 0).astype(BF16)
    return (
        result,
        d_tokens,
        d_gates,
        sum_gate.astype(BF16)[None],
        sum_up.astype(BF16)[None],
        sum_down.astype(BF16)[None],
    )


def solution(mesh):
    rows = P(("groups", "expert", "dp", "pair"), None)
    weights = P(("expert", "pair"), "dp", None)
    summed = P(("groups", "expert", "pair"), "dp", None)
    return jax.shard_map(
        per_device,
        mesh=mesh,
        in_specs=(rows, rows, rows, rows, weights, weights, weights),
        out_specs=(rows, rows, rows, summed, summed, summed),
        check_vma=False,
    )
```
